512 devices in a mesh: dp: 16 (over x_lo, z), tensor: 32 (over x_hi, y, core).
Axes of the slice: x: 4 (x_hi: 2, x_lo: 2; x = x_hi * 2 + x_lo), y: 8, z: 8, core: 2. Of those that a mesh axis runs over, the one named last changes fastest.
Arguments:
- activations: bfloat16 [2048, 28672], P('dp', 'tensor'), may hold values from -6 to 6
- cotangent: bfloat16 [2048, 8192], P('dp'), may hold values from -6 to 6
- weight: bfloat16 [28672, 8192], P('tensor', 'dp'), may hold values from -0.0625 to 0.0625
- clip_mask: int32 [2048, 28672], P('dp', 'tensor'), may hold values 0 or 1
- scale_exponent: int32 [2048], P('dp'), may hold values from -3 to 0
Outputs:
- input_gradient: bfloat16 [2048, 28672], P('dp', 'tensor')
- weight_gradient: bfloat16 [28672, 8192], P('tensor', 'dp')
The draws below stay inside these ranges and needn't reach their ends.
All inputs are finite; a program needn't handle non-finite values. No bound on the sum of `clip_mask` on one device may be relied on, other than what follows from the above.
Results may differ from the reference program's by a relative error of at most 0.027.
Values may be sent and summed in bfloat16 or wider, within the bound.
A program may use at most 64 MiB of HBM per device.

```python
import math
import jax
import jax.numpy as jnp
import numpy as np
from jax import lax

D = 8192
FF = 28672
TOKENS = 2048
N_DP = 16


def set_ends(entries, key, least, high):
    longest = entries.shape.index(max(entries.shape))
    spots = []
    for shift in (0, 1):
        where = [jax.random.randint(jax.random.fold_in(key, axis), (), 0, length) for axis, length in enumerate(entries.shape)]
        where[longest] = (where[longest] + shift) % entries.shape[longest]
        spots.append(tuple(where))
    return entries.at[spots[0]].set(least).at[spots[1]].set(high)


def with_spikes(values, key, source, target, blocks, factor):
    def block_of(position):
        return (jnp.arange(values.shape[position]) // (values.shape[position] // blocks)).reshape((-1,) + (1,) * (values.ndim - 1 - position))

    near = jax.random.permutation(key, blocks)[block_of(target)]
    other_side = (block_of(target) + blocks // 2) % blocks
    return jnp.where((block_of(source) == near) | (block_of(source) == other_side), factor * values, values)


def steps_of(stream_key, shape, shards, low, high):
    def one(position, parts):
        draws = jax.random.uniform(jax.random.fold_in(jax.random.fold_in(stream_key, 6), position), (parts,), jnp.float32, low / len(shards), high / len(shards))
        return jnp.repeat(jnp.exp(draws), shape[position] // parts).reshape((-1,) + (1,) * (len(shape) - position - 1))

    gain = one(*shards[0])
    for cut in shards[1:]:
        gain = gain * one(*cut)
    return gain


def normal_values(stream_key, shape, width, bound, cuts=(), kind=jnp.bfloat16):
    level = steps_of(stream_key, shape, cuts, -0.22, 0.18) if cuts else 1.0
    values = jax.random.normal(stream_key, shape, jnp.float32) * width * level
    return jnp.minimum(jnp.maximum(values, -bound), bound).astype(kind)


def heavy_noise(rng, extent, width, limit, cuts, heavy, kind=jnp.bfloat16):
    result = width * jax.random.normal(rng, extent, jnp.float32)
    if cuts:
        result = result * steps_of(rng, extent, cuts, -0.22, 0.18)
    return jnp.clip(with_spikes(result, jax.random.fold_in(rng, 3), *heavy), -limit, limit).astype(kind)


def setup_inputs(seed: int = 0) -> dict:
    keys = jax.random.split(jax.random.key(seed), 6)
    activations = normal_values(keys[0], (TOKENS, FF), 1.0, 6.0, ((0, 16), (1, 32)))
    cotangent = heavy_noise(keys[1], (TOKENS, D), 1.0, 6.0, ((0, 16),), (0, 1, 16, 2.0))
    weight = normal_values(keys[2], (FF, D), D ** -0.5, 0.0625, ((0, 32), (1, 16)))
    clip_mask = set_ends((jax.random.randint(keys[3], (TOKENS, FF), 0, 4) < 3).astype(jnp.int32), jax.random.fold_in(keys[3], 1), 0, 1)
    scale_exponent = set_ends(jax.random.randint(keys[4], (TOKENS,), -3, 1), jax.random.fold_in(keys[4], 1), -3, 0).astype(jnp.int32)
    return dict(activations=activations, cotangent=cotangent, weight=weight, clip_mask=clip_mask, scale_exponent=scale_exponent)


def paley_table():
    residues = set((number * number % 13 for number in range(1, 13)))
    jacobi = np.zeros((13, 13))
    for row_at in range(13):
        for col_at in range(13):
            differ = (col_at - row_at) % 13
            if differ != 0:
                jacobi[row_at, col_at] = 1.0 if differ in residues else -1.0
    confer = np.zeros((14, 14))
    confer[0, 1:] = 1.0
    confer[1:, 0] = 1.0
    confer[1:, 1:] = jacobi
    return np.kron(confer, np.array([[1.0, 1.0], [1.0, -1.0]])) + np.kron(np.eye(14), np.array([[1.0, -1.0], [-1.0, -1.0]]))

def sylvester_table(points):
    counter = np.arange(points)
    common = counter[:, None] & counter[None, :]
    parity = np.zeros((points, points), dtype=np.int64)
    for bit_pos in range(20):
        parity = parity + (common >> bit_pos & 1)
    return 1.0 - 2.0 * (parity % 2)

def rotate(values, transposed):
    outer = jnp.asarray(sylvester_table(FF // 28), jnp.float32)
    inner = jnp.asarray(paley_table(), jnp.float32)
    if transposed:
        outer = outer.T
        inner = inner.T
    framed = values.reshape(values.shape[0], FF // 28, 28)
    framed = jnp.einsum('nvw,vj->njw', framed, outer, precision=lax.Precision.HIGHEST)
    framed = jnp.einsum('njw,wk->njk', framed, inner, precision=lax.Precision.HIGHEST)
    return framed.reshape(values.shape) / math.sqrt(FF)

def reference(activations, cotangent, weight, clip_mask, scale_exponent):
    rotated = rotate(activations.astype(jnp.float32), False)
    step_size = jnp.exp2(scale_exponent.astype(jnp.float32))[:, None]
    quantized = jnp.clip(rotated, -8.0 * step_size, 7.0 * step_size).astype(jnp.bfloat16)
    block_width = D // N_DP
    grad_blocks = cotangent.reshape(TOKENS, N_DP, block_width).transpose(1, 0, 2)
    weight_blocks = weight.reshape(FF, N_DP, block_width).transpose(1, 0, 2)

    def add_block(running, pieces):
        term = lax.dot_general(pieces[0], pieces[1], (((1,), (1,)), ((), ())), preferred_element_type=jnp.float32)
        rounded = lax.optimization_barrier(term.astype(jnp.bfloat16))
        return (running + rounded.astype(jnp.float32), None)
    zero_total = jnp.zeros((TOKENS, FF), jnp.float32)
    grad_in, unused = lax.scan(add_block, zero_total, (grad_blocks, weight_blocks))
    masked = (clip_mask.astype(jnp.float32) * grad_in).astype(jnp.bfloat16)
    input_gradient = rotate(masked.astype(jnp.float32), True).astype(jnp.bfloat16)
    summed = jnp.dot(quantized.T, cotangent, preferred_element_type=jnp.float32)
    weight_gradient = (summed / math.sqrt(TOKENS)).astype(jnp.bfloat16)
    return (input_gradient, weight_gradient)
```

```python
import itertools
import math

import jax
import jax.numpy as jnp
import numpy as np
from jax import lax
from jax.experimental import pallas as pl
from jax.experimental.pallas import tpu as pltpu
from jax.sharding import PartitionSpec as P

FF = 28672
MESH = pl.DeviceIdType.MESH
BF = jnp.bfloat16
F32 = jnp.float32
TR = 16


def paley_table():
    residues = set((number * number % 13 for number in range(1, 13)))
    jacobi = np.zeros((13, 13))
    for row_at in range(13):
        for col_at in range(13):
            differ = (col_at - row_at) % 13
            if differ != 0:
                jacobi[row_at, col_at] = 1.0 if differ in residues else -1.0
    confer = np.zeros((14, 14))
    confer[0, 1:] = 1.0
    confer[1:, 0] = 1.0
    confer[1:, 1:] = jacobi
    return np.kron(confer, np.array([[1.0, 1.0], [1.0, -1.0]])) + np.kron(
        np.eye(14), np.array([[1.0, -1.0], [-1.0, -1.0]])
    )


def sylvester(points):
    counter = np.arange(points)
    common = counter[:, None] & counter[None, :]
    parity = np.zeros((points, points), np.int64)
    for bit_pos in range(points.bit_length()):
        parity = parity + (common >> bit_pos & 1)
    return 1.0 - 2.0 * (parity % 2)


class Chunk:
    pass


def chunk_scratch(Z, Y, R, DB, w):
    K = Z // 2
    slices = (Y, TR, w)
    return dict(
        f_own=((R, w), F32), f_s0=((R, w), BF), f_r0=((R, w), BF), f_s1=((R, w), BF), f_r1=((R, w), BF),
        f_as=(slices, BF), f_ar=(slices, BF), f_b=(slices, BF), q=((Z,) + slices, BF),
        xs=((w, DB), BF), xr=((w, DB), BF), wown=((w, DB), F32),
        g=((Z, R, w), F32), rs_s=((2, K, R, w), BF), rs_r=((2, K, R, w), BF),
        b_own=((R, w), F32), b_s0=((R, w), BF), b_r0=((R, w), BF), b_s1=((R, w), BF), b_r1=((R, w), BF),
        b_as=(slices, BF), b_ar=(slices, BF), b_b=(slices, BF), b_q=(slices, BF),
    )


def kernel(cfg, act_h, cot_h, w_h, mask_h, scale_v, table_h, gin_o, wg_o, *scr):
    Z, Y, R, F, DB, chunks, norm, wscale, order = cfg
    K, KY = Z // 2, Y // 2
    NC = len(chunks)
    scr = list(scr)
    act_v, table_v, mask_v, wbuf, cbuf, step_v, lsem, ssem, rsem = scr[:9]
    del scr[:9]
    ch = []
    at = 0
    for w in chunks:
        one = Chunk()
        one.lo, one.w = at, w
        at += w
        for name in chunk_scratch(Z, Y, R, DB, w):
            setattr(one, name, scr.pop(0))
        ch.append(one)

    dp, tn = lax.axis_index("dp"), lax.axis_index("tensor")
    xl, z = lax.div(dp, Z), lax.rem(dp, Z)
    xh, y, c = lax.div(tn, 2 * Y), lax.rem(lax.div(tn, 2), Y), lax.rem(tn, 2)

    def dev(xl_=xl, z_=z, xh_=xh, y_=y, c_=c):
        return {"dp": xl_ * Z + z_, "tensor": (xh_ * Y + y_) * 2 + c_}

    def zz(k):
        return lax.rem(z + (k + Z), Z)

    def yy(k):
        return lax.rem(y + (k + Y), Y)

    count, lcount = itertools.count(), itertools.count()
    sent = []

    def send(src, dst, to):
        k = next(count)
        copy = pltpu.make_async_remote_copy(
            src_ref=src, dst_ref=dst, send_sem=ssem.at[k], recv_sem=rsem.at[k], device_id=to, device_id_type=MESH
        )
        copy.start()
        sent.append(copy)
        return copy

    def local(src, dst):
        copy = pltpu.make_async_copy(src, dst, lsem.at[next(lcount)])
        copy.start()
        return copy

    def arrived(copies):
        for copy in copies:
            copy.wait_recv()

    sc, sh = (1 - 2 * c).astype(F32), (1 - 2 * xh).astype(F32)
    y_rows = pl.multiple_of(y * TR, TR)

    act_c = local(act_h, act_v)
    table_c = local(table_h, table_v)
    cot_c = local(
        cot_h.at[pl.ds(y_rows, TR), pl.ds(pl.multiple_of((c * Z + z) * DB, DB), DB)], cbuf.at[c, z, y]
    )
    mask_c = local(mask_h, mask_v)
    w_c = local(w_h, wbuf.at[xl])
    barrier = pltpu.get_barrier_semaphore()
    peers = [dev(c_=1 - c), dev(xh_=1 - xh), dev(xl_=1 - xl)]
    peers += [dev(y_=yy(k)) for k in range(1, Y)] + [dev(z_=zz(k)) for k in range(1, Z)]
    for peer in peers:
        pl.semaphore_signal(barrier, inc=1, device_id=peer, device_id_type=MESH)
    exponent = jnp.broadcast_to(scale_v[...], (R, R)).T
    step_v[...] = jnp.left_shift(jnp.ones_like(exponent), exponent + 3).astype(F32) * 0.125
    pl.semaphore_wait(barrier, len(peers))

    st = {}

    def cot_z():
        st["cz"] = [
            send(
                cot_h.at[pl.ds(y_rows, TR), pl.ds(pl.multiple_of((c * Z + zz(k)) * DB, DB), DB)],
                cbuf.at[c, z, y],
                dev(z_=zz(k)),
            )
            for k in range(1, Z)
        ]

    st["cc"] = []

    def core_share(view):
        st["cc"].append(send(view, view, dev(c_=1 - c)))

    def cot_y(s):
        if s == 0:
            cot_c.wait()
            arrived(st["cz"])
        else:
            arrived(st["cy"])
        if s < KY:
            last = s == KY - 1
            zr, zl = (pl.ds(0, Z // 2), pl.ds(Z // 2, Z // 2)) if last else (pl.ds(0, Z),) * 2
            right, left = cbuf.at[c, zr, yy(-s)], cbuf.at[c, zl, yy(s)]
            st["cy"] = [send(right, right, dev(y_=yy(1))), send(left, left, dev(y_=yy(-1)))]
        if s == 0:
            core_share(cbuf.at[c, :, y])
        elif s < KY:
            core_share(cbuf.at[c, :, yy(-s)])
            core_share(cbuf.at[c, :, yy(s)])
        else:
            core_share(cbuf.at[c, :, yy(s)])

    def cot_end():
        arrived(st["cc"])

    def weights(j):
        k = ch[j]
        rows = pl.ds(k.lo, k.w)
        k.wc = send(w_h.at[rows], wbuf.at[xl, rows], dev(xl_=1 - xl))

    def to_core(k, p, value):
        own, s0, r0 = getattr(k, p + "own"), getattr(k, p + "s0"), getattr(k, p + "r0")
        own[...] = value
        s0[...] = value.astype(BF)
        st[p, k, "c"] = [send(s0, r0, dev(c_=1 - c))]

    def to_xh(k, p):
        own, r0, s1, r1 = (getattr(k, p + n) for n in ("own", "r0", "s1", "r1"))
        arrived(st[p, k, "c"])
        value = r0[...].astype(F32) + sc * own[...]
        own[...] = value
        s1[...] = value.astype(BF)
        st[p, k, "x"] = [send(s1, r1, dev(xh_=1 - xh))]

    def to_y(k, p):
        own, r1, a_s, a_r = (getattr(k, p + n) for n in ("own", "r1", "as", "ar"))
        arrived(st[p, k, "x"])
        value = r1[...].astype(F32) + sh * own[...]
        a_s[...] = value.astype(BF).reshape(a_s.shape)
        st[p, k, "a"] = [send(a_s.at[yy(n)], a_r.at[y], dev(y_=yy(n))) for n in range(1, Y)]
        a_r[pl.ds(y, 1)] = a_s[pl.ds(y, 1)]

    def hada_y(k, p):
        a_r = getattr(k, p + "ar")
        arrived(st[p, k, "a"])
        parts = [a_r[n].astype(F32) for n in range(Y)]
        apart = 1
        while apart < Y:
            parts = [
                parts[n] + parts[n ^ apart] if not n & apart else parts[n ^ apart] - parts[n] for n in range(Y)
            ]
            apart *= 2
        return parts

    def back_y(k, p, target):
        b = getattr(k, p + "b")
        st[p, k, "b"] = [send(b.at[yy(n)], target.at[y], dev(y_=yy(n))) for n in range(1, Y)]
        target[pl.ds(y, 1)] = b[pl.ds(y, 1)]

    def f0(j):
        k = ch[j]
        if j == 0:
            act_c.wait()
            table_c.wait()
        to_core(k, "f_", jnp.dot(act_v[...], table_v[:, pl.ds(k.lo, k.w)], preferred_element_type=F32))

    def f1(j):
        to_xh(ch[j], "f_")

    def f2(j):
        to_y(ch[j], "f_")

    def f3(j):
        k = ch[j]
        parts = hada_y(k, "f_")
        step = step_v[pl.ds(y_rows, TR), :][:, 0:1]
        for n in range(Y):
            k.f_b[n] = jnp.clip(parts[n] * norm, -8.0 * step, 7.0 * step).astype(BF)
        back_y(k, "f_", k.q.at[z])

    def ag(j, s):
        k = ch[j]
        arrived(st["f_", k, "b"] if s == 0 else k.agc)
        if s < K:
            last = s == K - 1
            yr, yl = (pl.ds(0, Y // 2), pl.ds(Y // 2, Y // 2)) if last else (pl.ds(0, Y),) * 2
            right, left = k.q.at[zz(-s), yr], k.q.at[zz(s), yl]
            k.agc = [send(right, right, dev(z_=zz(1))), send(left, left, dev(z_=zz(-1)))]

    def wg_dot(k, half, out, cast):
        block = 128

        def step(n, _):
            cols = pl.ds(pl.multiple_of(n * block, block), block)
            rows = k.q[:, :, :, cols].reshape(Z * R, block)
            cot = cbuf[pl.ds(half, 1)].reshape(Z * R, DB)
            out[cols, :] = lax.dot_general(
                rows, cot, (((0,), (0,)), ((), ())), preferred_element_type=F32
            ).astype(cast)
            return _

        lax.fori_loop(0, k.w // block, step, 0)

    def wg(j):
        k = ch[j]
        wg_dot(k, 1 - xl, k.xs, BF)
        k.xc = send(k.xs, k.xr, dev(xl_=1 - xl))
        wg_dot(k, xl, k.wown, F32)

    def wend(j):
        k = ch[j]
        k.xc.wait_recv()
        wg_o[pl.ds(k.lo, k.w), :] = ((k.wown[...] + k.xr[...].astype(F32)) * wscale).astype(BF)

    def grad(j):
        k = ch[j]
        if j == 0:
            w_c.wait()
        k.wc.wait_recv()
        rows = pl.ds(k.lo, k.w)
        block = 2 if Z % 2 == 0 else 1

        def step(n, _):
            zs = pl.ds(n * block, block)
            total = jnp.zeros((block * R, k.w), F32)
            for half in range(2):
                total = total + lax.dot_general(
                    cbuf[half, zs].reshape(block * R, DB),
                    wbuf[half, rows, :],
                    (((1,), (1,)), ((), ())),
                    preferred_element_type=F32,
                )
            k.g[zs] = total.reshape(block, R, k.w)
            return _

        lax.fori_loop(0, Z // block, step, 0)

    top, bottom = pl.ds(0, R // 2), pl.ds(R // 2, R // 2)

    def rs(j, s):
        k = ch[j]
        if s == 0:
            for way, rows, to in ((0, top, 1), (1, bottom, -1)):
                k.rs_s[way, 0, rows, :] = k.g[zz(K), rows, :].astype(BF)
            k.rsc = [
                send(k.rs_s.at[way, 0, rows], k.rs_r.at[way, 0, rows], dev(z_=zz(to)))
                for way, rows, to in ((0, top, 1), (1, bottom, -1))
            ]
            return
        before = k.rsc
        k.rsc = []
        for way, rows, to in ((0, top, 1), (1, bottom, -1)):
            before[way].wait_recv()
            dest = zz(to * (K - s))
            if s == 1:
                other = bottom if way == 0 else top
                k.rs_s[way, 1, rows, :] = (k.g[dest, rows, :] + k.rs_r[way, 0, rows, :].astype(F32)).astype(BF)
                k.rs_s[way, 1, other, :] = k.g[dest, other, :].astype(BF)
            else:
                k.rs_s[way, s] = (k.g[dest] + k.rs_r[way, s - 1].astype(F32)).astype(BF)
            k.rsc.append(send(k.rs_s.at[way, s], k.rs_r.at[way, s], dev(z_=zz(to))))

    def b0(j):
        k = ch[j]
        if j == 0:
            mask_c.wait()
        arrived(k.rsc)
        total = k.g[z] + k.rs_r[0, K - 1].astype(F32) + k.rs_r[1, K - 1].astype(F32)
        mask = mask_v[:, pl.ds(k.lo, k.w)].astype(F32)
        to_core(k, "b_", (mask * total).astype(BF).astype(F32))

    def b1(j):
        to_xh(ch[j], "b_")

    def b2(j):
        to_y(ch[j], "b_")

    def b3(j):
        k = ch[j]
        parts = hada_y(k, "b_")
        for n in range(Y):
            k.b_b[n] = parts[n].astype(BF)
        back_y(k, "b_", k.b_q)

    def bend():
        total = jnp.zeros((R, F), F32)
        for k in ch:
            arrived(st["b_", k, "b"])
            total = total + jnp.dot(
                k.b_q[...].reshape(R, k.w), table_v[pl.ds(k.lo, k.w), :], preferred_element_type=F32
            )
        gin_o[...] = (total * norm).astype(BF)

    tasks = dict(locals())
    for name, *args in order(NC, K, KY):
        tasks[name](*args)
    for copy in sent:
        copy.wait_send()


def copies_of(NC, Z, Y):
    cot = (Z - 1) + 2 * (Y // 2) + Y
    each = 1 + 2 * (2 + 2 * (Y - 1)) + 4 * (Z // 2) + 1
    return cot + NC * each


def plan(NC, K, KY):
    J = range(NC)
    todo = [("cot_z",)]
    todo += [("f0", j) for j in J]
    todo += [("f1", j) for j in J]
    todo += [("weights", j) for j in J]
    todo += [("cot_y", 0)]
    todo += [("f2", j) for j in J]
    todo += [("cot_y", 1)]
    todo += [("f3", j) for j in J]
    todo += [("cot_y", s) for s in range(2, KY)]
    todo += [("ag", j, 0) for j in J]
    todo += [("cot_y", KY), ("cot_end",)]
    for j in J:
        todo += [("grad", j), ("rs", j, 0)]
    for s in range(1, K):
        todo += [("ag", j, s) for j in J]
        todo += [("rs", j, s) for j in J]
    for j in J:
        todo += [("b0", j), ("ag", j, K), ("wg", j)]
    todo += [("b1", j) for j in J]
    todo += [("b2", j) for j in J]
    todo += [("b3", j) for j in J]
    todo += [("bend",)]
    todo += [("wend", j) for j in J]
    return todo


def call(Z, Y, R, F, DB, chunks, norm, wscale, order, args):
    scratch = [
        pltpu.VMEM((R, F), BF), pltpu.VMEM((F, F), BF), pltpu.VMEM((R, F), jnp.int32),
        pltpu.VMEM((2, F, DB), BF), pltpu.VMEM((2, Z, Y, TR, DB), BF), pltpu.VMEM((R, R), F32),
        pltpu.SemaphoreType.DMA((5,)),
    ]
    total = copies_of(len(chunks), Z, Y)
    scratch += [pltpu.SemaphoreType.DMA((total,)), pltpu.SemaphoreType.DMA((total,))]
    for w in chunks:
        scratch += [pltpu.VMEM(*spec) for spec in chunk_scratch(Z, Y, R, DB, w).values()]
    cfg = (Z, Y, R, F, DB, chunks, norm, wscale, order)
    hbm, vmem = pl.BlockSpec(memory_space=pl.ANY), pl.BlockSpec(memory_space=pltpu.VMEM)

    def run(*refs):
        kernel(cfg, *refs)

    return pl.pallas_call(
        run,
        out_shape=(jax.ShapeDtypeStruct((R, F), BF), jax.ShapeDtypeStruct((F, DB), BF)),
        in_specs=[hbm, hbm, hbm, hbm, vmem, hbm],
        out_specs=(vmem, vmem),
        scratch_shapes=scratch,
        compiler_params=pltpu.CompilerParams(
            collective_id=0, has_side_effects=True, vmem_limit_bytes=52 * 2**20
        ),
    )(*args)


def body(activations, cotangent, weight, clip_mask, scale_exponent):
    R, F = activations.shape
    DB = weight.shape[1]
    table = jnp.asarray(np.kron(sylvester(F // 28), paley_table()), BF)
    tokens = R * lax.axis_size("dp")
    return call(
        8, 8, R, F, DB, (512, 384), 1.0 / math.sqrt(FF), 1.0 / math.sqrt(tokens), plan,
        (activations, cotangent, weight, clip_mask, scale_exponent.reshape(1, R), table),
    )


def solution(mesh):
    return jax.shard_map(
        body,
        mesh=mesh,
        in_specs=(P("dp", "tensor"), P("dp", None), P("tensor", "dp"), P("dp", "tensor"), P("dp")),
        out_specs=(P("dp", "tensor"), P("tensor", "dp")),
        check_vma=False,
    )
```

```python
import itertools
import math

import jax
import jax.numpy as jnp
import numpy as np
from jax import lax
from jax.experimental import pallas as pl
from jax.experimental.pallas import tpu as pltpu
from jax.sharding import PartitionSpec as P

FF = 28672
MESH = pl.DeviceIdType.MESH
BF = jnp.bfloat16
F32 = jnp.float32
TR = 16
PIECES = 4


def paley_table():
    residues = set((number * number % 13 for number in range(1, 13)))
    jacobi = np.zeros((13, 13))
    for row_at in range(13):
        for col_at in range(13):
            differ = (col_at - row_at) % 13
            if differ != 0:
                jacobi[row_at, col_at] = 1.0 if differ in residues else -1.0
    confer = np.zeros((14, 14))
    confer[0, 1:] = 1.0
    confer[1:, 0] = 1.0
    confer[1:, 1:] = jacobi
    return np.kron(confer, np.array([[1.0, 1.0], [1.0, -1.0]])) + np.kron(
        np.eye(14), np.array([[1.0, -1.0], [-1.0, -1.0]])
    )


def sylvester(points):
    counter = np.arange(points)
    common = counter[:, None] & counter[None, :]
    parity = np.zeros((points, points), np.int64)
    for bit_pos in range(points.bit_length()):
        parity = parity + (common >> bit_pos & 1)
    return 1.0 - 2.0 * (parity % 2)


class Chunk:
    pass


def padded(w):
    return -(-w // 256) * 256


def chunk_scratch(Z, Y, R, DB, w):
    K = Z // 2
    wide, half = (Y, TR, padded(w)), (2, Y, TR, padded(w) // 2)
    return dict(
        f_own=((R, w), F32), f_s0=((R, w), BF), f_r0=((R, w), BF),
        f_as=(wide, BF), f_ar=(half, BF), f_b=(half, BF), q=((Z,) + wide, BF),
        xs=((w, DB), BF), xr=((w, DB), BF), wown=((w, DB), F32),
        g=((Z, R, w), F32), rs_s=((2, K, R, w), BF), rs_r=((2, K, R, w), BF),
        b_own=((R, w), F32), b_s0=((R, w), BF), b_r0=((R, w), BF),
        b_as=(wide, BF), b_ar=(half, BF), b_b=(half, BF), b_q=(wide, BF),
    )


class Once:
    made = []

    def __init__(self, wait):
        self.run, self.done = wait, False
        Once.made.append(self)

    def wait(self):
        if not self.done:
            self.run()
        self.done = True


def kernel(cfg, act_h, cot_h, w_h, mask_h, scale_h, table_h, gin_o, wg_o, *scr):
    Z, Y, R, F, DB, chunks, norm, wscale, order = cfg
    K = Z // 2
    NC = len(chunks)
    scr = list(scr)
    act_v, table_v, mask_v, scale_v, wbuf, cbuf, step_v, gin_v, lsem, ssem, rsem = scr[:11]
    del scr[:11]
    ch = []
    at = 0
    for w in chunks:
        one = Chunk()
        one.lo, one.w, one.half = at, w, padded(w) // 2
        at += w
        for name in chunk_scratch(Z, Y, R, DB, w):
            setattr(one, name, scr.pop(0))
        ch.append(one)

    dp, tn = lax.axis_index("dp"), lax.axis_index("tensor")
    xl, z = lax.div(dp, Z), lax.rem(dp, Z)
    xh, y, c = lax.div(tn, 2 * Y), lax.rem(lax.div(tn, 2), Y), lax.rem(tn, 2)
    piece = lax.rem(y, PIECES)

    def dev(xl_=xl, z_=z, xh_=xh, y_=y, c_=c):
        return {"dp": xl_ * Z + z_, "tensor": (xh_ * Y + y_) * 2 + c_}

    def zz(k):
        return lax.rem(z + (k + Z), Z)

    def yy(k):
        return lax.rem(y + (k + Y), Y)

    count, lcount = itertools.count(), itertools.count()
    Once.made = []

    def send(src, dst, to):
        k = next(count)
        copy = pltpu.make_async_remote_copy(
            src_ref=src, dst_ref=dst, send_sem=ssem.at[k], recv_sem=rsem.at[k], device_id=to, device_id_type=MESH
        )
        copy.start()
        one = Once(copy.wait_recv)
        one.left = Once(copy.wait_send)
        return one

    def local(src, dst):
        copy = pltpu.make_async_copy(src, dst, lsem.at[next(lcount)])
        copy.start()
        return Once(copy.wait)

    def arrived(copies):
        for copy in copies:
            copy.wait()

    sc = (1 - 2 * c).astype(F32)
    y_rows = pl.multiple_of(y * TR, TR)
    far = sorted(range(Y), key=lambda n: -min(n, Y - n))
    others = [(h, n) for n in far for h in (1, 0) if (h, n) != (0, 0)]

    def mates(h):
        return 1 - xh if h else xh

    PR = R // PIECES
    mine = pl.multiple_of(piece * PR, PR)

    def cot_block(dest):
        return cot_h.at[pl.ds(mine, PR), pl.ds(pl.multiple_of((c * Z + dest) * DB, DB), DB)]

    scale_c = local(scale_h, scale_v)
    act_c = local(act_h, act_v)
    table_c = local(table_h, table_v)
    cot_c = local(cot_block(z), cbuf.at[c, z, pl.ds(mine, PR)])
    mask_c = local(mask_h, mask_v)
    w_c = local(w_h, wbuf.at[xl])
    barrier = pltpu.get_barrier_semaphore()
    peers = [dev(c_=1 - c), dev(xl_=1 - xl)]
    peers += [dev(xh_=mates(h), y_=yy(n)) for h, n in others] + [dev(z_=zz(k)) for k in range(1, Z)]
    for peer in peers:
        pl.semaphore_signal(barrier, inc=1, device_id=peer, device_id_type=MESH)
    for k in ch:
        if 2 * k.half > k.w:
            blank = jnp.zeros((Y, TR, 2 * k.half - k.w), BF)
            k.f_as[:, :, pl.ds(k.w, 2 * k.half - k.w)] = blank
            k.b_as[:, :, pl.ds(k.w, 2 * k.half - k.w)] = blank
    scale_c.wait()
    exponent = jnp.broadcast_to(scale_v[...], (R, R)).T
    step_v[...] = jnp.left_shift(jnp.ones_like(exponent), exponent + 3).astype(F32) * 0.125
    act_c.wait()
    table_c.wait()
    for k in ch:
        value = jnp.dot(act_v[...], table_v[:, pl.ds(k.lo, k.w)], preferred_element_type=F32)
        k.f_own[...] = value
        k.f_s0[...] = value.astype(BF)
    pl.semaphore_wait(barrier, len(peers))

    st = {}

    def cot_z():
        st["cz"] = {0: cot_c}
        for k in sorted(range(1, Z), key=lambda k: -min(k, Z - k)):
            st["cz"][k] = send(cot_block(zz(k)), cbuf.at[c, z, pl.ds(mine, PR)], dev(z_=zz(k)))

    st["cy"], st["cc"] = {}, {}

    def cot_fwd(k):
        st["cz"][k].wait()
        source = zz(-k)
        whole = cbuf.at[c, source, pl.ds(mine, PR)]
        first = cbuf.at[c, source, pl.ds(mine, PR // 2)]
        second = cbuf.at[c, source, pl.ds(pl.multiple_of(mine + PR // 2, PR // 2), PR // 2)]
        st["cy"][k] = [
            send(view, view, dev(y_=yy(n))) for view, n in ((first, 2), (second, -2), (whole, 1), (whole, -1))
        ]

    def cot_in(k):
        arrived(st["cy"][k])
        block = cbuf.at[c, zz(-k)]
        st["cc"][k] = send(block, block, dev(c_=1 - c))

    def weights(j):
        k = ch[j]
        rows = pl.ds(k.lo, k.w)
        if j > 0:
            ch[j - 1].wc.left.wait()
        k.wc = send(w_h.at[rows], wbuf.at[xl, rows], dev(xl_=1 - xl))

    def to_core(k, p):
        st[p, k, "c"] = [send(getattr(k, p + "s0"), getattr(k, p + "r0"), dev(c_=1 - c))]

    def lanes(k, h):
        return pl.ds(pl.multiple_of(mates(h) * k.half, 128), k.half)

    def to_y(k, p):
        own, r0, a_s, a_r = (getattr(k, p + n) for n in ("own", "r0", "as", "ar"))
        arrived(st[p, k, "c"])
        value = r0[...].astype(F32) + sc * own[...]
        a_s[:, :, pl.ds(0, k.w)] = value.astype(BF).reshape(Y, TR, k.w)
        st[p, k, "a"] = [
            send(a_s.at[yy(n), :, lanes(k, h)], a_r.at[xh, y], dev(xh_=mates(h), y_=yy(n))) for h, n in others
        ]
        own_rows = a_s[pl.ds(y, 1)]
        a_r[pl.ds(xh, 1), pl.ds(y, 1)] = jnp.where(xh == 0, own_rows[:, :, : k.half], own_rows[:, :, k.half :])[None]

    def hada(k, p):
        a_r = getattr(k, p + "ar")
        arrived(st[p, k, "a"])
        parts = [a_r[n // Y, n % Y].astype(F32) for n in range(2 * Y)]
        apart = 1
        while apart < 2 * Y:
            parts = [
                parts[n] + parts[n ^ apart] if not n & apart else parts[n ^ apart] - parts[n] for n in range(2 * Y)
            ]
            apart *= 2
        return parts

    def back_y(k, p, target):
        b = getattr(k, p + "b")
        st[p, k, "b"] = [
            send(b.at[mates(h), yy(n)], target.at[y, :, lanes(k, 0)], dev(xh_=mates(h), y_=yy(n))) for h, n in others
        ]
        for h in range(2):

            @pl.when(xh == h)
            def _():
                target[pl.ds(y, 1), :, pl.ds(h * k.half, k.half)] = b[h, pl.ds(y, 1)]

    def f0(j):
        to_core(ch[j], "f_")

    def f1(j):
        to_y(ch[j], "f_")

    def f2(j):
        k = ch[j]
        parts = hada(k, "f_")
        step = step_v[pl.ds(y_rows, TR), :][:, 0:1]
        for n in range(2 * Y):
            k.f_b[n // Y, n % Y] = jnp.clip(parts[n] * norm, -8.0 * step, 7.0 * step).astype(BF)
        back_y(k, "f_", k.q.at[z])

    def ag(j, s):
        k = ch[j]
        arrived(st["f_", k, "b"] if s == 0 else k.agc)
        if s < K:
            last = s == K - 1
            yr, yl = (pl.ds(0, Y // 2), pl.ds(Y // 2, Y // 2)) if last else (pl.ds(0, Y),) * 2
            cols = pl.ds(0, k.w)
            right, left = k.q.at[zz(-s), yr, :, cols], k.q.at[zz(s), yl, :, cols]
            k.agc = [send(right, right, dev(z_=zz(1))), send(left, left, dev(z_=zz(-1)))]

    def wg_dot(k, half, cast):
        rows = k.q[:, :, :, pl.ds(0, k.w)].reshape(Z * R, k.w)
        cot = cbuf[pl.ds(half, 1)].reshape(Z * R, DB)
        return lax.dot_general(rows, cot, (((0,), (0,)), ((), ())), preferred_element_type=F32).astype(cast)

    def wg(j):
        k = ch[j]
        arrived(st["cc"].values())
        k.xs[...] = wg_dot(k, 1 - xl, BF)
        k.xc = send(k.xs, k.xr, dev(xl_=1 - xl))
        k.wown[...] = wg_dot(k, xl, F32)

    def wend(j):
        k = ch[j]
        k.xc.wait()
        wg_o[pl.ds(k.lo, k.w), :] = ((k.wown[...] + k.xr[...].astype(F32)) * wscale).astype(BF)

    def grad(j, s):
        k = ch[j]
        w_c.wait()
        k.wc.wait()
        for near in {(K - s) % Z, (s - K) % Z}:
            st["cc"][near].wait()
        rows = pl.ds(k.lo, k.w)
        dests = [zz(K - s)] if s in (0, K) else [zz(K - s), zz(s - K)]
        total = None
        for half in range(2):
            cot = jnp.concatenate([cbuf[half, pl.ds(dest, 1)].reshape(R, DB) for dest in dests], 0)
            part = lax.dot_general(cot, wbuf[half, rows, :], (((1,), (1,)), ((), ())), preferred_element_type=F32)
            total = part if total is None else total + part
        for n, dest in enumerate(dests):
            k.g[pl.ds(dest, 1)] = total[n * R : (n + 1) * R][None]

    top, bottom = pl.ds(0, R // 2), pl.ds(R // 2, R // 2)

    def rs(j, s):
        k = ch[j]
        if s == 0:
            for way, rows, to in ((0, top, 1), (1, bottom, -1)):
                k.rs_s[way, 0, rows, :] = k.g[zz(K), rows, :].astype(BF)
            k.rsc = [
                send(k.rs_s.at[way, 0, rows], k.rs_r.at[way, 0, rows], dev(z_=zz(to)))
                for way, rows, to in ((0, top, 1), (1, bottom, -1))
            ]
            return
        before = k.rsc
        k.rsc = []
        for way, rows, to in ((0, top, 1), (1, bottom, -1)):
            before[way].wait()
            dest = zz(to * (K - s))
            if s == 1:
                other = bottom if way == 0 else top
                k.rs_s[way, 1, rows, :] = (k.g[dest, rows, :] + k.rs_r[way, 0, rows, :].astype(F32)).astype(BF)
                k.rs_s[way, 1, other, :] = k.g[dest, other, :].astype(BF)
            else:
                k.rs_s[way, s] = (k.g[dest] + k.rs_r[way, s - 1].astype(F32)).astype(BF)
            k.rsc.append(send(k.rs_s.at[way, s], k.rs_r.at[way, s], dev(z_=zz(to))))

    def b0(j):
        k = ch[j]
        mask_c.wait()
        arrived(k.rsc)
        total = k.g[z] + k.rs_r[0, K - 1].astype(F32) + k.rs_r[1, K - 1].astype(F32)
        mask = mask_v[:, pl.ds(k.lo, k.w)].astype(F32)
        masked = (mask * total).astype(BF)
        k.b_own[...] = masked.astype(F32)
        k.b_s0[...] = masked
        to_core(k, "b_")

    def b1(j):
        to_y(ch[j], "b_")

    def b2(j):
        k = ch[j]
        parts = hada(k, "b_")
        for n in range(2 * Y):
            k.b_b[n // Y, n % Y] = parts[n].astype(BF)
        back_y(k, "b_", k.b_q)

    def b3(j):
        k = ch[j]
        arrived(st["b_", k, "b"])
        part = jnp.dot(
            k.b_q[:, :, pl.ds(0, k.w)].reshape(R, k.w), table_v[pl.ds(k.lo, k.w), :], preferred_element_type=F32
        )
        if j > 0:
            part = part + gin_v[...]
        if j < NC - 1:
            gin_v[...] = part
        else:
            gin_o[...] = (part * norm).astype(BF)

    tasks = dict(locals())
    for name, *args in order(NC, Z):
        tasks[name](*args)
    for one in Once.made:
        one.wait()


def copies_of(NC, Z, Y):
    cot = (Z - 1) + 5 * Z
    each = 1 + 2 * (1 + 2 * (2 * Y - 1)) + 4 * (Z // 2) + 1
    return cot + NC * each


STEPS = (
    ('f0', 1), ('cot_z',), ('f0', 0), ('f1', 1), ('f1', 0), ('cot_fwd', 7), ('weights', 0), ('f0', 2), ('f1', 2),
    ('cot_fwd', 2), ('cot_fwd', 1), ('f2', 0), ('f2', 1), ('f2', 2), ('weights', 1), ('cot_fwd', 6),
    ('cot_fwd', 5), ('ag', 0, 0), ('cot_in', 2), ('cot_in', 1), ('cot_fwd', 4), ('ag', 1, 0), ('cot_in', 5),
    ('cot_fwd', 3), ('ag', 0, 1), ('cot_in', 4), ('ag', 2, 0), ('cot_in', 6), ('weights', 2), ('ag', 1, 1),
    ('cot_in', 3), ('grad', 0, 0), ('cot_in', 7), ('rs', 0, 0), ('grad', 1, 0), ('rs', 1, 0), ('cot_fwd', 0),
    ('ag', 2, 1), ('grad', 1, 1), ('grad', 0, 1), ('ag', 1, 2), ('rs', 0, 1), ('grad', 0, 2), ('grad', 1, 3),
    ('grad', 0, 3), ('grad', 1, 2), ('grad', 2, 0), ('rs', 2, 0), ('rs', 1, 1), ('grad', 2, 3), ('cot_in', 0),
    ('ag', 1, 3), ('rs', 0, 2), ('grad', 2, 1), ('grad', 2, 2), ('grad', 0, 4), ('rs', 2, 1), ('grad', 2, 4),
    ('ag', 2, 2), ('ag', 1, 4), ('rs', 1, 2), ('wg', 1), ('rs', 0, 3), ('rs', 2, 2), ('rs', 1, 3), ('grad', 1, 4),
    ('rs', 2, 3), ('ag', 2, 3), ('b0', 0), ('b1', 0), ('b0', 1), ('b1', 1), ('b0', 2), ('ag', 0, 2), ('ag', 2, 4),
    ('wg', 2), ('b1', 2), ('b2', 0), ('ag', 0, 3), ('b2', 1), ('b2', 2), ('ag', 0, 4), ('wg', 0), ('b3', 0),
    ('wend', 1), ('b3', 1), ('b3', 2), ('wend', 2), ('wend', 0),
)


def plan(NC, Z):
    return STEPS


def call(Z, Y, R, F, DB, chunks, norm, wscale, order, args):
    scratch = [
        pltpu.VMEM((R, F), BF), pltpu.VMEM((F, F), BF), pltpu.VMEM((R, F), jnp.int32), pltpu.VMEM((1, R), jnp.int32),
        pltpu.VMEM((2, F, DB), BF), pltpu.VMEM((2, Z, R, DB), BF), pltpu.VMEM((R, R), F32), pltpu.VMEM((R, F), F32),
        pltpu.SemaphoreType.DMA((6,)),
    ]
    total = copies_of(len(chunks), Z, Y)
    scratch += [pltpu.SemaphoreType.DMA((total,)), pltpu.SemaphoreType.DMA((total,))]
    for w in chunks:
        scratch += [pltpu.VMEM(*spec) for spec in chunk_scratch(Z, Y, R, DB, w).values()]
    cfg = (Z, Y, R, F, DB, chunks, norm, wscale, order)
    hbm, vmem = pl.BlockSpec(memory_space=pltpu.HBM), pl.BlockSpec(memory_space=pltpu.VMEM)

    def run(*refs):
        kernel(cfg, *refs)

    return pl.pallas_call(
        run,
        out_shape=(jax.ShapeDtypeStruct((R, F), BF), jax.ShapeDtypeStruct((F, DB), BF)),
        in_specs=[hbm] * 6,
        out_specs=(vmem, vmem),
        scratch_shapes=scratch,
        compiler_params=pltpu.CompilerParams(
            collective_id=0, has_side_effects=True, vmem_limit_bytes=52 * 2**20
        ),
    )(*args)


def body(activations, cotangent, weight, clip_mask, scale_exponent):
    R, F = activations.shape
    DB = weight.shape[1]
    table = jnp.asarray(np.kron(sylvester(F // 28), paley_table()), BF)
    tokens = R * lax.axis_size("dp")
    return call(
        8, 8, R, F, DB, (256, 384, 256), 1.0 / math.sqrt(FF), 1.0 / math.sqrt(tokens), plan,
        (activations, cotangent, weight, clip_mask, scale_exponent.reshape(1, R), table),
    )


def solution(mesh):
    return jax.shard_map(
        body,
        mesh=mesh,
        in_specs=(P("dp", "tensor"), P("dp", None), P("tensor", "dp"), P("dp", "tensor"), P("dp")),
        out_specs=(P("dp", "tensor"), P("tensor", "dp")),
        check_vma=False,
    )
```

```python
import itertools
import math

import jax
import jax.numpy as jnp
import numpy as np
from jax import lax
from jax.experimental import pallas as pl
from jax.experimental.pallas import tpu as pltpu
from jax.sharding import PartitionSpec as P

FF = 28672
MESH = pl.DeviceIdType.MESH
BF = jnp.bfloat16
F32 = jnp.float32
TR = 16
PIECES = 4


def paley_table():
    residues = set((number * number % 13 for number in range(1, 13)))
    jacobi = np.zeros((13, 13))
    for row_at in range(13):
        for col_at in range(13):
            differ = (col_at - row_at) % 13
            if differ != 0:
                jacobi[row_at, col_at] = 1.0 if differ in residues else -1.0
    confer = np.zeros((14, 14))
    confer[0, 1:] = 1.0
    confer[1:, 0] = 1.0
    confer[1:, 1:] = jacobi
    return np.kron(confer, np.array([[1.0, 1.0], [1.0, -1.0]])) + np.kron(
        np.eye(14), np.array([[1.0, -1.0], [-1.0, -1.0]])
    )


def sylvester(points):
    counter = np.arange(points)
    common = counter[:, None] & counter[None, :]
    parity = np.zeros((points, points), np.int64)
    for bit_pos in range(points.bit_length()):
        parity = parity + (common >> bit_pos & 1)
    return 1.0 - 2.0 * (parity % 2)


class Chunk:
    pass


def padded(w):
    return -(-w // 256) * 256


def group_scratch(Z, Y, R, w):
    wide, half = (Y, TR, padded(w)), (2, Y, TR, padded(w) // 2)
    return dict(
        f_own=((R, w), F32), f_s0=((R, w), BF), f_r0=((R, w), BF),
        f_as=(wide, BF), f_ar=(half, BF), f_b=(half, BF), q=((Z,) + wide, BF),
        b_own=((R, w), F32), b_s0=((R, w), BF), b_r0=((R, w), BF),
        b_as=(wide, BF), b_ar=(half, BF), b_b=(half, BF), b_q=(wide, BF),
    )


def chunk_scratch(Z, R, DB, w):
    K = Z // 2
    return dict(
        xs=((w, DB), BF), xr=((w, DB), BF), wown=((w, DB), F32),
        g=((Z, R, w), F32), rs_s=((2, K, R, w), BF), rs_r=((2, K, R, w), BF),
    )


class Once:
    made = []

    def __init__(self, wait):
        self.run, self.done = wait, False
        Once.made.append(self)

    def wait(self):
        if not self.done:
            self.run()
        self.done = True


def kernel(cfg, act_h, cot_h, w_h, mask_h, scale_h, table_h, gin_o, wg_o, *scr):
    Z, Y, R, F, DB, chunks, norm, wscale, order = cfg
    K = Z // 2
    NG = len(chunks)
    scr = list(scr)
    act_v, table_v, mask_v, scale_v, wbuf, cbuf, step_v, gin_v, lsem, ssem, rsem = scr[:11]
    del scr[:11]
    ch, groups = [], []
    at = 0
    for widths in chunks:
        group = Chunk()
        group.lo, group.w, group.half, group.parts = at, sum(widths), padded(sum(widths)) // 2, []
        for name in group_scratch(Z, Y, R, group.w):
            setattr(group, name, scr.pop(0))
        groups.append(group)
        for w in widths:
            one = Chunk()
            one.lo, one.w, one.group, one.cols = at, w, group, pl.ds(at - group.lo, w)
            at += w
            for name in chunk_scratch(Z, R, DB, w):
                setattr(one, name, scr.pop(0))
            group.parts.append(one)
            ch.append(one)

    dp, tn = lax.axis_index("dp"), lax.axis_index("tensor")
    xl, z = lax.div(dp, Z), lax.rem(dp, Z)
    xh, y, c = lax.div(tn, 2 * Y), lax.rem(lax.div(tn, 2), Y), lax.rem(tn, 2)
    piece = lax.rem(y, PIECES)

    def dev(xl_=xl, z_=z, xh_=xh, y_=y, c_=c):
        return {"dp": xl_ * Z + z_, "tensor": (xh_ * Y + y_) * 2 + c_}

    def zz(k):
        return lax.rem(z + (k + Z), Z)

    def yy(k):
        return lax.rem(y + (k + Y), Y)

    count, lcount = itertools.count(), itertools.count()
    Once.made = []

    def send(src, dst, to):
        k = next(count)
        copy = pltpu.make_async_remote_copy(
            src_ref=src, dst_ref=dst, send_sem=ssem.at[k], recv_sem=rsem.at[k], device_id=to, device_id_type=MESH
        )
        copy.start()
        one = Once(copy.wait_recv)
        one.left = Once(copy.wait_send)
        return one

    def local(src, dst):
        copy = pltpu.make_async_copy(src, dst, lsem.at[next(lcount)])
        copy.start()
        return Once(copy.wait)

    def arrived(copies):
        for copy in copies:
            copy.wait()

    sc = (1 - 2 * c).astype(F32)
    y_rows = pl.multiple_of(y * TR, TR)
    far = sorted(range(Y), key=lambda n: -min(n, Y - n))
    others = [(h, n) for n in far for h in (1, 0) if (h, n) != (0, 0)]

    def mates(h):
        return 1 - xh if h else xh

    PR = R // PIECES
    mine = pl.multiple_of(piece * PR, PR)

    def cot_block(dest):
        return cot_h.at[pl.ds(mine, PR), pl.ds(pl.multiple_of((c * Z + dest) * DB, DB), DB)]

    scale_c = local(scale_h, scale_v)
    act_c = local(act_h, act_v)
    table_c = local(table_h, table_v)
    cot_c = local(cot_block(z), cbuf.at[c, z, pl.ds(mine, PR)])
    mask_c = local(mask_h, mask_v)
    w_c = local(w_h, wbuf.at[xl])
    barrier = pltpu.get_barrier_semaphore()
    peers = [dev(c_=1 - c), dev(xl_=1 - xl)]
    peers += [dev(xh_=mates(h), y_=yy(n)) for h, n in others] + [dev(z_=zz(k)) for k in range(1, Z)]
    for peer in peers:
        pl.semaphore_signal(barrier, inc=1, device_id=peer, device_id_type=MESH)
    for k in groups:
        if 2 * k.half > k.w:
            blank = jnp.zeros((Y, TR, 2 * k.half - k.w), BF)
            k.f_as[:, :, pl.ds(k.w, 2 * k.half - k.w)] = blank
            k.b_as[:, :, pl.ds(k.w, 2 * k.half - k.w)] = blank
    scale_c.wait()
    exponent = jnp.broadcast_to(scale_v[...], (R, R)).T
    step_v[...] = jnp.left_shift(jnp.ones_like(exponent), exponent + 3).astype(F32) * 0.125
    act_c.wait()
    table_c.wait()
    for k in groups:
        value = jnp.dot(act_v[...], table_v[:, pl.ds(k.lo, k.w)], preferred_element_type=F32)
        k.f_own[...] = value
        k.f_s0[...] = value.astype(BF)
    pl.semaphore_wait(barrier, len(peers))

    st = {}

    def cot_z():
        st["cz"] = {0: cot_c}
        for k in sorted(range(1, Z), key=lambda k: -min(k, Z - k)):
            st["cz"][k] = send(cot_block(zz(k)), cbuf.at[c, z, pl.ds(mine, PR)], dev(z_=zz(k)))

    st["cy"], st["cc"] = {}, {}

    def cot_fwd(k):
        st["cz"][k].wait()
        source = zz(-k)
        whole = cbuf.at[c, source, pl.ds(mine, PR)]
        first = cbuf.at[c, source, pl.ds(mine, PR // 2)]
        second = cbuf.at[c, source, pl.ds(pl.multiple_of(mine + PR // 2, PR // 2), PR // 2)]
        st["cy"][k] = [
            send(view, view, dev(y_=yy(n))) for view, n in ((first, 2), (second, -2), (whole, 1), (whole, -1))
        ]

    def cot_in(k):
        arrived(st["cy"][k])
        block = cbuf.at[c, zz(-k)]
        st["cc"][k] = send(block, block, dev(c_=1 - c))

    def weights(j):
        k = ch[j]
        rows = pl.ds(k.lo, k.w)
        if j > 0:
            ch[j - 1].wc.left.wait()
        k.wc = send(w_h.at[rows], wbuf.at[xl, rows], dev(xl_=1 - xl))

    def to_core(k, p, cols):
        source, target = getattr(k, p + "s0").at[:, cols], getattr(k, p + "r0").at[:, cols]
        st.setdefault((p, k, "c"), []).append(send(source, target, dev(c_=1 - c)))

    def lanes(k, h):
        return pl.ds(pl.multiple_of(mates(h) * k.half, 128), k.half)

    def to_y(k, p):
        own, r0, a_s, a_r = (getattr(k, p + n) for n in ("own", "r0", "as", "ar"))
        arrived(st[p, k, "c"])
        value = r0[...].astype(F32) + sc * own[...]
        a_s[:, :, pl.ds(0, k.w)] = value.astype(BF).reshape(Y, TR, k.w)
        st[p, k, "a"] = [
            send(a_s.at[yy(n), :, lanes(k, h)], a_r.at[xh, y], dev(xh_=mates(h), y_=yy(n))) for h, n in others
        ]
        own_rows = a_s[pl.ds(y, 1)]
        a_r[pl.ds(xh, 1), pl.ds(y, 1)] = jnp.where(xh == 0, own_rows[:, :, : k.half], own_rows[:, :, k.half :])[None]

    def hada(k, p):
        a_r = getattr(k, p + "ar")
        arrived(st[p, k, "a"])
        parts = [a_r[n // Y, n % Y].astype(F32) for n in range(2 * Y)]
        apart = 1
        while apart < 2 * Y:
            parts = [
                parts[n] + parts[n ^ apart] if not n & apart else parts[n ^ apart] - parts[n] for n in range(2 * Y)
            ]
            apart *= 2
        return parts

    def back_y(k, p, target):
        b = getattr(k, p + "b")
        st[p, k, "b"] = [
            send(b.at[mates(h), yy(n)], target.at[y, :, lanes(k, 0)], dev(xh_=mates(h), y_=yy(n))) for h, n in others
        ]
        for h in range(2):

            @pl.when(xh == h)
            def _():
                target[pl.ds(y, 1), :, pl.ds(h * k.half, k.half)] = b[h, pl.ds(y, 1)]

    def f0(j):
        to_core(groups[j], "f_", pl.ds(0, groups[j].w))

    def f1(j):
        to_y(groups[j], "f_")

    def f2(j):
        k = groups[j]
        parts = hada(k, "f_")
        step = step_v[pl.ds(y_rows, TR), :][:, 0:1]
        for n in range(2 * Y):
            k.f_b[n // Y, n % Y] = jnp.clip(parts[n] * norm, -8.0 * step, 7.0 * step).astype(BF)
        back_y(k, "f_", k.q.at[z])

    def ag(j, s):
        k = ch[j]
        arrived(st["f_", k.group, "b"] if s == 0 else k.agc)
        if s < K:
            last = s == K - 1
            yr, yl = (pl.ds(0, Y // 2), pl.ds(Y // 2, Y // 2)) if last else (pl.ds(0, Y),) * 2
            q = k.group.q
            right, left = q.at[zz(-s), yr, :, k.cols], q.at[zz(s), yl, :, k.cols]
            k.agc = [send(right, right, dev(z_=zz(1))), send(left, left, dev(z_=zz(-1)))]

    def wg_dot(k, half, cast):
        rows = k.group.q[:, :, :, k.cols].reshape(Z * R, k.w)
        cot = cbuf[pl.ds(half, 1)].reshape(Z * R, DB)
        return lax.dot_general(rows, cot, (((0,), (0,)), ((), ())), preferred_element_type=F32).astype(cast)

    def wg(j):
        k = ch[j]
        arrived(st["cc"].values())
        k.xs[...] = wg_dot(k, 1 - xl, BF)
        k.xc = send(k.xs, k.xr, dev(xl_=1 - xl))
        k.wown[...] = wg_dot(k, xl, F32)

    def wend(j):
        k = ch[j]
        k.xc.wait()
        wg_o[pl.ds(k.lo, k.w), :] = ((k.wown[...] + k.xr[...].astype(F32)) * wscale).astype(BF)

    def grad(j, s):
        k = ch[j]
        w_c.wait()
        k.wc.wait()
        for near in {(K - s) % Z, (s - K) % Z}:
            st["cc"][near].wait()
        rows = pl.ds(k.lo, k.w)
        dests = [zz(K - s)] if s in (0, K) else [zz(K - s), zz(s - K)]
        total = None
        for half in range(2):
            cot = jnp.concatenate([cbuf[half, pl.ds(dest, 1)].reshape(R, DB) for dest in dests], 0)
            part = lax.dot_general(cot, wbuf[half, rows, :], (((1,), (1,)), ((), ())), preferred_element_type=F32)
            total = part if total is None else total + part
        for n, dest in enumerate(dests):
            k.g[pl.ds(dest, 1)] = total[n * R : (n + 1) * R][None]

    top, bottom = pl.ds(0, R // 2), pl.ds(R // 2, R // 2)

    def rs(j, s):
        k = ch[j]
        if s == 0:
            for way, rows, to in ((0, top, 1), (1, bottom, -1)):
                k.rs_s[way, 0, rows, :] = k.g[zz(K), rows, :].astype(BF)
            k.rsc = [
                send(k.rs_s.at[way, 0, rows], k.rs_r.at[way, 0, rows], dev(z_=zz(to)))
                for way, rows, to in ((0, top, 1), (1, bottom, -1))
            ]
            return
        before = k.rsc
        k.rsc = []
        for way, rows, to in ((0, top, 1), (1, bottom, -1)):
            before[way].wait()
            dest = zz(to * (K - s))
            if s == 1:
                other = bottom if way == 0 else top
                k.rs_s[way, 1, rows, :] = (k.g[dest, rows, :] + k.rs_r[way, 0, rows, :].astype(F32)).astype(BF)
                k.rs_s[way, 1, other, :] = k.g[dest, other, :].astype(BF)
            else:
                k.rs_s[way, s] = (k.g[dest] + k.rs_r[way, s - 1].astype(F32)).astype(BF)
            k.rsc.append(send(k.rs_s.at[way, s], k.rs_r.at[way, s], dev(z_=zz(to))))

    def b0(j):
        k = ch[j]
        mask_c.wait()
        arrived(k.rsc)
        total = k.g[z] + k.rs_r[0, K - 1].astype(F32) + k.rs_r[1, K - 1].astype(F32)
        mask = mask_v[:, pl.ds(k.lo, k.w)].astype(F32)
        masked = (mask * total).astype(BF)
        k.group.b_own[:, k.cols] = masked.astype(F32)
        k.group.b_s0[:, k.cols] = masked
        to_core(k.group, "b_", k.cols)

    def b1(j):
        to_y(groups[j], "b_")

    def b2(j):
        k = groups[j]
        parts = hada(k, "b_")
        for n in range(2 * Y):
            k.b_b[n // Y, n % Y] = parts[n].astype(BF)
        back_y(k, "b_", k.b_q)

    def b3(j):
        k = groups[j]
        arrived(st["b_", k, "b"])
        part = jnp.dot(
            k.b_q[:, :, pl.ds(0, k.w)].reshape(R, k.w), table_v[pl.ds(k.lo, k.w), :], preferred_element_type=F32
        )
        if j > 0:
            part = part + gin_v[...]
        if j < NG - 1:
            gin_v[...] = part
        else:
            gin_o[...] = (part * norm).astype(BF)

    tasks = dict(locals())
    for name, *args in order:
        tasks[name](*args)
    for one in Once.made:
        one.wait()


def copies_of(chunks, Z, Y):
    cot = (Z - 1) + 5 * Z
    group = 1 + 4 * (2 * Y - 1)
    return cot + len(chunks) * group + sum(map(len, chunks)) * (1 + 4 * (Z // 2) + 2)


STEPS = (
    ('cot_z',), ('weights', 0), ('f0', 0), ('cot_fwd', 0), ('f1', 0), ('f0', 1), ('weights', 1), ('cot_in', 0),
    ('f1', 1), ('cot_fwd', 6), ('f2', 0), ('cot_in', 6), ('cot_fwd', 4), ('cot_fwd', 3), ('cot_fwd', 2),
    ('weights', 2), ('ag', 0, 0), ('f2', 1), ('ag', 1, 0), ('cot_in', 2), ('cot_in', 4), ('ag', 0, 1),
    ('cot_in', 3), ('cot_fwd', 5), ('grad', 0, 2), ('grad', 0, 0), ('rs', 0, 0), ('grad', 1, 0), ('ag', 1, 1),
    ('grad', 0, 4), ('rs', 1, 0), ('cot_fwd', 1), ('cot_fwd', 7), ('grad', 2, 0), ('rs', 2, 0), ('ag', 0, 2),
    ('ag', 2, 0), ('cot_in', 5), ('ag', 1, 2), ('grad', 2, 2), ('grad', 0, 1), ('rs', 0, 1), ('grad', 2, 1),
    ('cot_in', 1), ('grad', 1, 1), ('rs', 1, 1), ('cot_in', 7), ('rs', 2, 1), ('grad', 0, 3), ('ag', 1, 3),
    ('ag', 0, 3), ('rs', 0, 2), ('grad', 1, 2), ('rs', 1, 2), ('rs', 2, 2), ('ag', 1, 4), ('ag', 2, 1),
    ('ag', 0, 4), ('grad', 1, 3), ('rs', 0, 3), ('wg', 0), ('grad', 2, 4), ('rs', 1, 3), ('grad', 2, 3), ('wg', 1),
    ('grad', 1, 4), ('rs', 2, 3), ('ag', 2, 2), ('b0', 0), ('b0', 1), ('b1', 0), ('b0', 2), ('ag', 2, 3),
    ('b1', 1), ('ag', 2, 4), ('wg', 2), ('b2', 0), ('wend', 0), ('wend', 1), ('b2', 1), ('b3', 0), ('wend', 2),
    ('b3', 1),
)


def call(Z, Y, R, F, DB, chunks, norm, wscale, order, args):
    scratch = [
        pltpu.VMEM((R, F), BF), pltpu.VMEM((F, F), BF), pltpu.VMEM((R, F), jnp.int32), pltpu.VMEM((1, R), jnp.int32),
        pltpu.VMEM((2, F, DB), BF), pltpu.VMEM((2, Z, R, DB), BF), pltpu.VMEM((R, R), F32), pltpu.VMEM((R, F), F32),
        pltpu.SemaphoreType.DMA((6,)),
    ]
    total = copies_of(chunks, Z, Y)
    scratch += [pltpu.SemaphoreType.DMA((total,)), pltpu.SemaphoreType.DMA((total,))]
    for widths in chunks:
        scratch += [pltpu.VMEM(*spec) for spec in group_scratch(Z, Y, R, sum(widths)).values()]
        for w in widths:
            scratch += [pltpu.VMEM(*spec) for spec in chunk_scratch(Z, R, DB, w).values()]
    cfg = (Z, Y, R, F, DB, chunks, norm, wscale, order)
    hbm, vmem = pl.BlockSpec(memory_space=pltpu.HBM), pl.BlockSpec(memory_space=pltpu.VMEM)

    def run(*refs):
        kernel(cfg, *refs)

    args = [pltpu.with_memory_space_constraint(arg, pltpu.HBM) for arg in args]

    return pl.pallas_call(
        run,
        out_shape=(jax.ShapeDtypeStruct((R, F), BF), jax.ShapeDtypeStruct((F, DB), BF)),
        in_specs=[hbm] * 6,
        out_specs=(vmem, vmem),
        scratch_shapes=scratch,
        compiler_params=pltpu.CompilerParams(
            collective_id=0, has_side_effects=True, vmem_limit_bytes=52 * 2**20
        ),
    )(*args)


def body(activations, cotangent, weight, clip_mask, scale_exponent):
    R, F = activations.shape
    DB = weight.shape[1]
    table = jnp.asarray(np.kron(sylvester(F // 28), paley_table()), BF)
    tokens = R * lax.axis_size("dp")
    return call(
        8, 8, R, F, DB, ((256, 256), (384,)), 1.0 / math.sqrt(FF), 1.0 / math.sqrt(tokens), STEPS,
        (activations, cotangent, weight, clip_mask, scale_exponent.reshape(1, R), table),
    )


def solution(mesh):
    return jax.shard_map(
        body,
        mesh=mesh,
        in_specs=(P("dp", "tensor"), P("dp", None), P("tensor", "dp"), P("dp", "tensor"), P("dp")),
        out_specs=(P("dp", "tensor"), P("tensor", "dp")),
        check_vma=False,
    )
```

```python
import itertools
import math

import jax
import jax.numpy as jnp
import numpy as np
from jax import lax
from jax.experimental import pallas as pl
from jax.experimental.pallas import tpu as pltpu
from jax.sharding import PartitionSpec as P

FF = 28672
MESH = pl.DeviceIdType.MESH
BF = jnp.bfloat16
F32 = jnp.float32
TR = 16
PIECES = 4


def paley_table():
    residues = set((number * number % 13 for number in range(1, 13)))
    jacobi = np.zeros((13, 13))
    for row_at in range(13):
        for col_at in range(13):
            differ = (col_at - row_at) % 13
            if differ != 0:
                jacobi[row_at, col_at] = 1.0 if differ in residues else -1.0
    confer = np.zeros((14, 14))
    confer[0, 1:] = 1.0
    confer[1:, 0] = 1.0
    confer[1:, 1:] = jacobi
    return np.kron(confer, np.array([[1.0, 1.0], [1.0, -1.0]])) + np.kron(
        np.eye(14), np.array([[1.0, -1.0], [-1.0, -1.0]])
    )


def sylvester(points):
    counter = np.arange(points)
    common = counter[:, None] & counter[None, :]
    parity = np.zeros((points, points), np.int64)
    for bit_pos in range(points.bit_length()):
        parity = parity + (common >> bit_pos & 1)
    return 1.0 - 2.0 * (parity % 2)


class Chunk:
    pass


def padded(w):
    return -(-w // 256) * 256


def group_scratch(Z, Y, R, w):
    wide, half = (Y, TR, padded(w)), (2, Y, TR, padded(w) // 2)
    return dict(
        f_own=((R, w), F32), f_s0=((R, w), BF), f_r0=((R, w), BF),
        f_as=(wide, BF), f_ar=(half, BF), f_b=(half, BF), q=((Z,) + wide, BF),
        b_own=((R, w), F32), b_s0=((R, w), BF), b_r0=((R, w), BF),
        b_as=(wide, BF), b_ar=(half, BF), b_b=(half, BF), b_q=(wide, BF),
    )


def chunk_scratch(Z, R, DB, w):
    K = Z // 2
    return dict(
        xs=((w, DB), BF), xr=((w, DB), BF), wown=((w, DB), F32),
        g=((Z, R, w), F32), rs_s=((2, K, R, w), BF), rs_r=((2, K, R, w), BF),
    )


class Once:
    made = []

    def __init__(self, wait):
        self.run, self.done = wait, False
        Once.made.append(self)

    def wait(self):
        if not self.done:
            self.run()
        self.done = True


def kernel(cfg, act_h, cot_h, w_h, mask_h, scale_h, table_h, gin_o, wg_o, *scr):
    Z, Y, R, F, DB, chunks, norm, wscale, order = cfg
    K = Z // 2
    NG = len(chunks)
    scr = list(scr)
    act_v, table_v, mask_v, scale_v, wbuf, cbuf, step_v, gin_v, lsem, ssem, rsem = scr[:11]
    del scr[:11]
    ch, groups = [], []
    at = 0
    for widths in chunks:
        group = Chunk()
        group.lo, group.w, group.half, group.parts = at, sum(widths), padded(sum(widths)) // 2, []
        for name in group_scratch(Z, Y, R, group.w):
            setattr(group, name, scr.pop(0))
        groups.append(group)
        for w in widths:
            one = Chunk()
            one.lo, one.w, one.group, one.cols = at, w, group, pl.ds(at - group.lo, w)
            at += w
            for name in chunk_scratch(Z, R, DB, w):
                setattr(one, name, scr.pop(0))
            group.parts.append(one)
            ch.append(one)

    dp, tn = lax.axis_index("dp"), lax.axis_index("tensor")
    xl, z = lax.div(dp, Z), lax.rem(dp, Z)
    xh, y, c = lax.div(tn, 2 * Y), lax.rem(lax.div(tn, 2), Y), lax.rem(tn, 2)
    piece = lax.rem(y, PIECES)

    def dev(xl_=xl, z_=z, xh_=xh, y_=y, c_=c):
        return {"dp": xl_ * Z + z_, "tensor": (xh_ * Y + y_) * 2 + c_}

    def zz(k):
        return lax.rem(z + (k + Z), Z)

    def yy(k):
        return lax.rem(y + (k + Y), Y)

    count, lcount = itertools.count(), itertools.count()
    Once.made = []

    def send(src, dst, to):
        k = next(count)
        copy = pltpu.make_async_remote_copy(
            src_ref=src, dst_ref=dst, send_sem=ssem.at[k], recv_sem=rsem.at[k], device_id=to, device_id_type=MESH
        )
        copy.start()
        one = Once(copy.wait_recv)
        one.left = Once(copy.wait_send)
        return one

    def local(src, dst):
        copy = pltpu.make_async_copy(src, dst, lsem.at[next(lcount)])
        copy.start()
        return Once(copy.wait)

    def arrived(copies):
        for copy in copies:
            copy.wait()

    sc = (1 - 2 * c).astype(F32)
    y_rows = pl.multiple_of(y * TR, TR)
    far = sorted(range(Y), key=lambda n: -min(n, Y - n))
    others = [(h, n) for n in far for h in (1, 0) if (h, n) != (0, 0)]

    def mates(h):
        return 1 - xh if h else xh

    PR = R // PIECES
    mine = pl.multiple_of(piece * PR, PR)

    def cot_block(dest):
        return cot_h.at[pl.ds(mine, PR), pl.ds(pl.multiple_of((c * Z + dest) * DB, DB), DB)]

    scale_c = local(scale_h, scale_v)
    act_c = local(act_h, act_v)
    table_c = local(table_h, table_v)
    cot_c = local(cot_block(z), cbuf.at[c, z, pl.ds(mine, PR)])
    mask_c = local(mask_h, mask_v)
    w_c = local(w_h, wbuf.at[xl])
    barrier = pltpu.get_barrier_semaphore()
    peers = [dev(c_=1 - c), dev(xl_=1 - xl)]
    peers += [dev(xh_=mates(h), y_=yy(n)) for h, n in others] + [dev(z_=zz(k)) for k in range(1, Z)]
    for peer in peers:
        pl.semaphore_signal(barrier, inc=1, device_id=peer, device_id_type=MESH)
    for k in groups:
        if 2 * k.half > k.w:
            blank = jnp.zeros((Y, TR, 2 * k.half - k.w), BF)
            k.f_as[:, :, pl.ds(k.w, 2 * k.half - k.w)] = blank
            k.b_as[:, :, pl.ds(k.w, 2 * k.half - k.w)] = blank
    scale_c.wait()
    exponent = jnp.broadcast_to(scale_v[...], (R, R)).T
    step_v[...] = jnp.left_shift(jnp.ones_like(exponent), exponent + 3).astype(F32) * 0.125
    act_c.wait()
    table_c.wait()
    for k in groups:
        value = jnp.dot(act_v[...], table_v[:, pl.ds(k.lo, k.w)], preferred_element_type=F32)
        k.f_own[...] = value
        k.f_s0[...] = value.astype(BF)
    pl.semaphore_wait(barrier, len(peers))

    st = {}

    def cot_z():
        st["cz"] = {0: cot_c}
        for k in sorted(range(1, Z), key=lambda k: -min(k, Z - k)):
            st["cz"][k] = send(cot_block(zz(k)), cbuf.at[c, z, pl.ds(mine, PR)], dev(z_=zz(k)))

    st["cy"], st["cc"] = {}, {}

    def cot_fwd(k):
        st["cz"][k].wait()
        source = zz(-k)
        whole = cbuf.at[c, source, pl.ds(mine, PR)]
        first = cbuf.at[c, source, pl.ds(mine, PR // 2)]
        second = cbuf.at[c, source, pl.ds(pl.multiple_of(mine + PR // 2, PR // 2), PR // 2)]
        st["cy"][k] = [
            send(view, view, dev(y_=yy(n))) for view, n in ((first, 2), (second, -2), (whole, 1), (whole, -1))
        ]

    def cot_in(k):
        arrived(st["cy"][k])
        block = cbuf.at[c, zz(-k)]
        st["cc"][k] = send(block, block, dev(c_=1 - c))

    def weights(j):
        k = ch[j]
        rows = pl.ds(k.lo, k.w)
        if j > 0:
            ch[j - 1].wc.left.wait()
        k.wc = send(w_h.at[rows], wbuf.at[xl, rows], dev(xl_=1 - xl))

    def to_core(k, p, cols):
        source, target = getattr(k, p + "s0").at[:, cols], getattr(k, p + "r0").at[:, cols]
        st.setdefault((p, k, "c"), []).append(send(source, target, dev(c_=1 - c)))

    def lanes(k, h):
        return pl.ds(pl.multiple_of(mates(h) * k.half, 128), k.half)

    def to_y(k, p):
        own, r0, a_s, a_r = (getattr(k, p + n) for n in ("own", "r0", "as", "ar"))
        arrived(st[p, k, "c"])
        value = r0[...].astype(F32) + sc * own[...]
        a_s[:, :, pl.ds(0, k.w)] = value.astype(BF).reshape(Y, TR, k.w)
        st[p, k, "a"] = [
            send(a_s.at[yy(n), :, lanes(k, h)], a_r.at[xh, y], dev(xh_=mates(h), y_=yy(n))) for h, n in others
        ]
        own_rows = a_s[pl.ds(y, 1)]
        a_r[pl.ds(xh, 1), pl.ds(y, 1)] = jnp.where(xh == 0, own_rows[:, :, : k.half], own_rows[:, :, k.half :])[None]

    def hada(k, p):
        a_r = getattr(k, p + "ar")
        arrived(st[p, k, "a"])
        parts = [a_r[n // Y, n % Y].astype(F32) for n in range(2 * Y)]
        apart = 1
        while apart < 2 * Y:
            parts = [
                parts[n] + parts[n ^ apart] if not n & apart else parts[n ^ apart] - parts[n] for n in range(2 * Y)
            ]
            apart *= 2
        return parts

    def back_y(k, p, target):
        b = getattr(k, p + "b")
        st[p, k, "b"] = [
            send(b.at[mates(h), yy(n)], target.at[y, :, lanes(k, 0)], dev(xh_=mates(h), y_=yy(n))) for h, n in others
        ]
        for h in range(2):

            @pl.when(xh == h)
            def _():
                target[pl.ds(y, 1), :, pl.ds(h * k.half, k.half)] = b[h, pl.ds(y, 1)]

    def f0(j):
        to_core(groups[j], "f_", pl.ds(0, groups[j].w))

    def f1(j):
        to_y(groups[j], "f_")

    def f2(j):
        k = groups[j]
        parts = hada(k, "f_")
        step = step_v[pl.ds(y_rows, TR), :][:, 0:1]
        for n in range(2 * Y):
            k.f_b[n // Y, n % Y] = jnp.clip(parts[n] * norm, -8.0 * step, 7.0 * step).astype(BF)
        back_y(k, "f_", k.q.at[z])

    def ag(j, s):
        k = ch[j]
        arrived(st["f_", k.group, "b"] if s == 0 else k.agc)
        if s < K:
            last = s == K - 1
            yr, yl = (pl.ds(0, Y // 2), pl.ds(Y // 2, Y // 2)) if last else (pl.ds(0, Y),) * 2
            q = k.group.q
            right, left = q.at[zz(-s), yr, :, k.cols], q.at[zz(s), yl, :, k.cols]
            k.agc = [send(right, right, dev(z_=zz(1))), send(left, left, dev(z_=zz(-1)))]

    def wg_dot(k, half, cast):
        rows = k.group.q[:, :, :, k.cols].reshape(Z * R, k.w)
        cot = cbuf[pl.ds(half, 1)].reshape(Z * R, DB)
        return lax.dot_general(rows, cot, (((0,), (0,)), ((), ())), preferred_element_type=F32).astype(cast)

    def wg(j):
        k = ch[j]
        arrived(st["cc"].values())
        k.xs[...] = wg_dot(k, 1 - xl, BF)
        k.xc = send(k.xs, k.xr, dev(xl_=1 - xl))
        k.wown[...] = wg_dot(k, xl, F32)

    def wend(j):
        k = ch[j]
        k.xc.wait()
        wg_o[pl.ds(k.lo, k.w), :] = ((k.wown[...] + k.xr[...].astype(F32)) * wscale).astype(BF)

    def grad(j, s):
        k = ch[j]
        w_c.wait()
        k.wc.wait()
        for near in {(K - s) % Z, (s - K) % Z}:
            st["cc"][near].wait()
        rows = pl.ds(k.lo, k.w)
        dests = [zz(K - s)] if s in (0, K) else [zz(K - s), zz(s - K)]
        total = None
        for half in range(2):
            cot = jnp.concatenate([cbuf[half, pl.ds(dest, 1)].reshape(R, DB) for dest in dests], 0)
            part = lax.dot_general(cot, wbuf[half, rows, :], (((1,), (1,)), ((), ())), preferred_element_type=F32)
            total = part if total is None else total + part
        for n, dest in enumerate(dests):
            k.g[pl.ds(dest, 1)] = total[n * R : (n + 1) * R][None]

    top, bottom = pl.ds(0, R // 2), pl.ds(R // 2, R // 2)

    def rs(j, s):
        k = ch[j]
        if s == 0:
            for way, rows, to in ((0, top, 1), (1, bottom, -1)):
                k.rs_s[way, 0, rows, :] = k.g[zz(K), rows, :].astype(BF)
            k.rsc = [
                send(k.rs_s.at[way, 0, rows], k.rs_r.at[way, 0, rows], dev(z_=zz(to)))
                for way, rows, to in ((0, top, 1), (1, bottom, -1))
            ]
            return
        before = k.rsc
        k.rsc = []
        for way, rows, to in ((0, top, 1), (1, bottom, -1)):
            before[way].wait()
            dest = zz(to * (K - s))
            if s == 1:
                other = bottom if way == 0 else top
                k.rs_s[way, 1, rows, :] = (k.g[dest, rows, :] + k.rs_r[way, 0, rows, :].astype(F32)).astype(BF)
                k.rs_s[way, 1, other, :] = k.g[dest, other, :].astype(BF)
            else:
                k.rs_s[way, s] = (k.g[dest] + k.rs_r[way, s - 1].astype(F32)).astype(BF)
            k.rsc.append(send(k.rs_s.at[way, s], k.rs_r.at[way, s], dev(z_=zz(to))))

    def b0(j):
        k = ch[j]
        mask_c.wait()
        arrived(k.rsc)
        total = k.g[z] + k.rs_r[0, K - 1].astype(F32) + k.rs_r[1, K - 1].astype(F32)
        mask = mask_v[:, pl.ds(k.lo, k.w)].astype(F32)
        masked = (mask * total).astype(BF)
        k.group.b_own[:, k.cols] = masked.astype(F32)
        k.group.b_s0[:, k.cols] = masked
        to_core(k.group, "b_", k.cols)

    def b1(j):
        to_y(groups[j], "b_")

    def b2(j):
        k = groups[j]
        parts = hada(k, "b_")
        for n in range(2 * Y):
            k.b_b[n // Y, n % Y] = parts[n].astype(BF)
        back_y(k, "b_", k.b_q)

    def b3(j):
        k = groups[j]
        arrived(st["b_", k, "b"])
        part = jnp.dot(
            k.b_q[:, :, pl.ds(0, k.w)].reshape(R, k.w), table_v[pl.ds(k.lo, k.w), :], preferred_element_type=F32
        )
        if j > 0:
            part = part + gin_v[...]
        if j < NG - 1:
            gin_v[...] = part
        else:
            gin_o[...] = (part * norm).astype(BF)

    tasks = dict(locals())
    for name, *args in order:
        tasks[name](*args)
    for one in Once.made:
        one.wait()


def copies_of(chunks, Z, Y):
    cot = (Z - 1) + 5 * Z
    group = 1 + 4 * (2 * Y - 1)
    return cot + len(chunks) * group + sum(map(len, chunks)) * (1 + 4 * (Z // 2) + 2)


STEPS = (
    ('f0', 0), ('weights', 0), ('cot_z',), ('cot_fwd', 0), ('f0', 1), ('f1', 0), ('weights', 1), ('f1', 1),
    ('f2', 0), ('cot_fwd', 4), ('f2', 1), ('weights', 2), ('ag', 0, 0), ('cot_fwd', 2), ('cot_fwd', 5),
    ('cot_fwd', 3), ('cot_fwd', 6), ('cot_in', 0), ('ag', 1, 0), ('ag', 0, 1), ('ag', 2, 0), ('cot_in', 4),
    ('grad', 0, 0), ('ag', 1, 1), ('grad', 1, 0), ('rs', 1, 0), ('cot_fwd', 1), ('grad', 2, 0), ('cot_fwd', 7),
    ('ag', 0, 2), ('cot_in', 2), ('rs', 2, 0), ('rs', 0, 0), ('cot_in', 6), ('cot_in', 3), ('cot_in', 5),
    ('ag', 2, 1), ('grad', 2, 1), ('grad', 0, 4), ('grad', 0, 1), ('ag', 1, 2), ('grad', 1, 2), ('cot_in', 1),
    ('grad', 1, 1), ('rs', 1, 1), ('rs', 0, 1), ('cot_in', 7), ('grad', 1, 4), ('ag', 0, 3), ('grad', 1, 3),
    ('rs', 2, 1), ('grad', 0, 2), ('grad', 0, 3), ('ag', 1, 3), ('grad', 2, 2), ('ag', 2, 2), ('grad', 2, 4),
    ('rs', 1, 2), ('ag', 0, 4), ('wg', 0), ('rs', 0, 2), ('rs', 2, 2), ('rs', 1, 3), ('ag', 1, 4), ('rs', 0, 3),
    ('grad', 2, 3), ('rs', 2, 3), ('ag', 2, 3), ('wg', 1), ('b0', 1), ('b0', 0), ('b1', 0), ('b0', 2), ('wend', 0),
    ('b1', 1), ('ag', 2, 4), ('wg', 2), ('b2', 0), ('wend', 1), ('b2', 1), ('b3', 0), ('wend', 2), ('b3', 1),
)


def call(Z, Y, R, F, DB, chunks, norm, wscale, order, args):
    scratch = [
        pltpu.VMEM((R, F), BF), pltpu.VMEM((F, F), BF), pltpu.VMEM((R, F), jnp.int32), pltpu.VMEM((1, R), jnp.int32),
        pltpu.VMEM((2, F, DB), BF), pltpu.VMEM((2, Z, R, DB), BF), pltpu.VMEM((R, R), F32), pltpu.VMEM((R, F), F32),
        pltpu.SemaphoreType.DMA((6,)),
    ]
    total = copies_of(chunks, Z, Y)
    scratch += [pltpu.SemaphoreType.DMA((total,)), pltpu.SemaphoreType.DMA((total,))]
    for widths in chunks:
        scratch += [pltpu.VMEM(*spec) for spec in group_scratch(Z, Y, R, sum(widths)).values()]
        for w in widths:
            scratch += [pltpu.VMEM(*spec) for spec in chunk_scratch(Z, R, DB, w).values()]
    cfg = (Z, Y, R, F, DB, chunks, norm, wscale, order)
    hbm, vmem = pl.BlockSpec(memory_space=pltpu.HBM), pl.BlockSpec(memory_space=pltpu.VMEM)

    def run(*refs):
        kernel(cfg, *refs)

    args = [pltpu.with_memory_space_constraint(arg, pltpu.HBM) for arg in args]

    return pl.pallas_call(
        run,
        out_shape=(jax.ShapeDtypeStruct((R, F), BF), jax.ShapeDtypeStruct((F, DB), BF)),
        in_specs=[hbm] * 6,
        out_specs=(vmem, vmem),
        scratch_shapes=scratch,
        compiler_params=pltpu.CompilerParams(
            collective_id=0, has_side_effects=True, vmem_limit_bytes=52 * 2**20
        ),
    )(*args)


def body(activations, cotangent, weight, clip_mask, scale_exponent):
    R, F = activations.shape
    DB = weight.shape[1]
    table = jnp.asarray(np.kron(sylvester(F // 28), paley_table()), BF)
    tokens = R * lax.axis_size("dp")
    return call(
        8, 8, R, F, DB, ((256, 256), (384,)), 1.0 / math.sqrt(FF), 1.0 / math.sqrt(tokens), STEPS,
        (activations, cotangent, weight, clip_mask, scale_exponent.reshape(1, R), table),
    )


def solution(mesh):
    return jax.shard_map(
        body,
        mesh=mesh,
        in_specs=(P("dp", "tensor"), P("dp", None), P("tensor", "dp"), P("dp", "tensor"), P("dp")),
        out_specs=(P("dp", "tensor"), P("tensor", "dp")),
        check_vma=False,
    )
```
